32 devices in a mesh: comp: 2 (over core), seq: 8 (over z, y), tp: 2 (over x).
Axes of the slice: x: 2, y: 2, z: 4, core: 2. Of those that a mesh axis runs over, the one named last changes fastest.
Arguments:
- inputs: bfloat16 [2, 8, 1024, 3072], P('comp', None, ('seq', 'tp')), may hold values from -6 to 6
- modulation: float32 [2, 8, 3, 3072], P('comp'), may hold values from -4 to 4
- w_qkv: bfloat16 [2, 3072, 3, 3072], P('comp', None, None, 'tp'), may hold values from -0.108253175 to 0.108253175
- w_attn_out: bfloat16 [2, 3072, 3072], P('comp', 'tp'), may hold values from -0.109375 to 0.109375
- qk_gain: float32 [2, 2, 128], P('comp'), may hold values from 1 to 5
- final_mod: float32 [8, 2, 3072], replicated, may hold values from -4 to 4
- w_final: bfloat16 [3072, 64], replicated, may hold values from -0.109375 to 0.109375
- w_embed: bfloat16 [64, 3072], replicated, may hold values from -0.75 to 0.75
- latent: float32 [8, 64, 1024], P(None, None, ('seq', 'tp')), may hold values from -6 to 6
Outputs:
- handed: bfloat16 [2, 8, 1024, 3072], P('comp', None, ('seq', 'tp'))
- velocity: float32 [8, 64, 1024], P(None, None, ('seq', 'tp'))
- advanced: float32 [8, 64, 1024], P(None, None, ('seq', 'tp'))
The draws below stay inside these ranges and needn't reach their ends.
All inputs are finite; a program needn't handle non-finite values.
Results may differ from the reference program's by a relative error of at most 0.011.
Values may be sent and summed in bfloat16 or wider, within the bound.
A program may use at most 256 MiB of HBM per device.

```python
import math
import jax
import jax.numpy as jnp
from jax import lax

D = 3072
HEADS = 24
HD = 128
CL = 64
SAMPLES = 8
COMP = 2
TOKENS = 1024


def draw_w_qkv(key, part):
    base = jax.random.truncated_normal(key, -5.9, 5.9, (COMP, D, 3, D), jnp.float32) * D ** (-0.5)
    return base.astype(jnp.bfloat16)


def draw_qk_gain(key, part):
    low_end, high_end = (math.log(1.2), math.log(2.2))
    return jnp.exp(jax.random.uniform(key, (COMP, 2, HD), jnp.float32, low_end, high_end))


def block_scale(rng, extent, split, smallest, high):
    def one(dim, blocks):
        steps = jax.random.uniform(jax.random.fold_in(jax.random.fold_in(rng, 6), dim), (blocks,), jnp.float32, smallest / len(split), high / len(split))
        return jnp.repeat(jnp.exp(steps), extent[dim] // blocks).reshape((-1,) + (1,) * (len(extent) - dim - 1))

    level = one(*split[0])
    for cut in split[1:]:
        level = level * one(*cut)
    return level


def normal_values(stream_key, extent, scale, limit, split=(), held_as=jnp.bfloat16):
    values = scale * jax.random.normal(stream_key, extent, jnp.float32)
    if split:
        values = values * block_scale(stream_key, extent, split, -0.22, 0.18)
    return jnp.clip(values, -limit, limit).astype(held_as)


def setup_inputs(seed: int = 0) -> dict:
    splits = jax.random.split(jax.random.key(seed), 10)
    inputs = normal_values(splits[0], (COMP, SAMPLES, TOKENS, D), 1.0, 6.0, ((0, 2), (2, 16)))
    modulation = normal_values(splits[1], (COMP, SAMPLES, 3, D), 0.8, 4.0, ((0, 2),), jnp.float32)
    w_qkv = draw_w_qkv(jax.random.fold_in(splits[9], 71), 0)
    w_attn_out = normal_values(splits[3], (COMP, D, D), D ** -0.5, 0.109375, ((0, 2), (1, 2)))
    qk_gain = draw_qk_gain(jax.random.fold_in(splits[9], 71), 0)
    final_mod = normal_values(splits[5], (SAMPLES, 2, D), 0.8, 4.0, (), jnp.float32)
    w_final = normal_values(splits[6], (D, CL), D ** -0.5, 0.109375)
    w_embed = normal_values(splits[7], (CL, D), CL ** -0.5, 0.75)
    latent = normal_values(splits[8], (SAMPLES, CL, TOKENS), 1.0, 6.0, ((2, 16),), jnp.float32)
    return {"inputs": inputs, "modulation": modulation, "w_qkv": w_qkv, "w_attn_out": w_attn_out, "qk_gain": qk_gain, "final_mod": final_mod, "w_final": w_final, "w_embed": w_embed, "latent": latent}


step_size = 0.02
norm_eps = 1e-06

def layer_norm(values):
    center = values - lax.optimization_barrier(jnp.mean(values, -1, keepdims=True))
    return center * lax.rsqrt(lax.optimization_barrier(jnp.mean(center * center, -1, keepdims=True)) + norm_eps)

def rms_norm(values, norm_gain):
    return values * lax.rsqrt(lax.optimization_barrier(jnp.mean(values * values, -1, keepdims=True)) + norm_eps) * norm_gain

def attend(queried, keyed_rows, valued):
    scaling = HD ** (-0.5)
    block_rows = math.gcd(TOKENS, 512)
    keys_float = keyed_rows.astype(jnp.float32)
    values_float = valued.astype(jnp.float32)

    def one_block(query_block):
        scores = jnp.einsum('qhd,khd->qhk', query_block.astype(jnp.float32), keys_float) * scaling
        row_max = lax.optimization_barrier(jnp.max(scores, -1, keepdims=True))
        weight = jnp.exp(scores - row_max)
        weight_sum = lax.optimization_barrier(jnp.sum(weight, -1))
        rounded = lax.optimization_barrier(weight.astype(jnp.bfloat16)).astype(jnp.float32)
        summed = jnp.einsum('qhk,khd->qhd', rounded, values_float)
        return (summed / weight_sum[..., None]).astype(jnp.bfloat16)
    blocks = lax.map(one_block, queried.reshape(TOKENS // block_rows, block_rows, HEADS, HD))
    return blocks.reshape(TOKENS, HEADS, HD)

def component(x_rows, mod_rows, weights, out_weights, norm_gains):
    x_float = x_rows.astype(jnp.float32)
    x_mod = (layer_norm(x_float) * (1.0 + mod_rows[:, 1, None, :]) + mod_rows[:, 0, None, :]).astype(jnp.bfloat16)
    mixed_rows = jnp.dot(x_mod.reshape(SAMPLES * TOKENS, D), weights.reshape(D, 3 * D), preferred_element_type=jnp.float32)
    mixed_rows = mixed_rows.reshape(SAMPLES, TOKENS, 3, HEADS, HD)
    queried = rms_norm(mixed_rows[:, :, 0], norm_gains[0]).astype(jnp.bfloat16)
    keyed_rows = rms_norm(mixed_rows[:, :, 1], norm_gains[1]).astype(jnp.bfloat16)
    valued = mixed_rows[:, :, 2].astype(jnp.bfloat16)
    attended = lax.map(lambda packed: attend(*packed), (queried, keyed_rows, valued))
    branch = jnp.dot(attended.reshape(SAMPLES * TOKENS, D), out_weights, preferred_element_type=jnp.float32)
    branch = branch.reshape(SAMPLES, TOKENS, D)
    return (x_float + mod_rows[:, 2, None, :] * branch).astype(jnp.bfloat16)

def reference(inputs, modulation, w_qkv, w_attn_out, qk_gain, final_mod, w_final, w_embed, latent):
    outputs = lax.map(lambda packed: component(*packed), (inputs, modulation, w_qkv, w_attn_out, qk_gain))
    last_out = outputs[COMP - 1].astype(jnp.float32)
    final_in = (layer_norm(last_out) * (1.0 + final_mod[:, 1, None, :]) + final_mod[:, 0, None, :]).astype(jnp.bfloat16)
    projected = jnp.dot(final_in.reshape(SAMPLES * TOKENS, D), w_final, preferred_element_type=jnp.float32)
    velocity = projected.reshape(SAMPLES, TOKENS, CL).transpose(0, 2, 1)
    advanced = latent + step_size * velocity
    flat_latent = advanced.transpose(0, 2, 1).reshape(SAMPLES * TOKENS, CL).astype(jnp.bfloat16)
    embedded = jnp.dot(flat_latent, w_embed, preferred_element_type=jnp.float32).astype(jnp.bfloat16)
    embedded = embedded.reshape(SAMPLES, TOKENS, D)
    handed = jnp.concatenate([embedded[None], outputs[:-1]], 0)
    return (handed, velocity, advanced)
```

```python
import jax
import jax.numpy as jnp
from jax import lax
from jax.sharding import PartitionSpec as P

step_size = 0.02
norm_eps = 1e-06


def broadcast(block, axis, owner):
    block = jnp.where(lax.axis_index(axis) == owner, block, jnp.zeros_like(block))
    return lax.psum(block, axis)


def shifted(block, axis, distance):
    devices = range(lax.axis_size(axis))
    route = [((i - distance) % len(devices), i) for i in devices]
    return lax.ppermute(block, axis, route)


def layer_norm(values):
    center = values - jnp.mean(values, -1, keepdims=True)
    return center * lax.rsqrt(jnp.mean(center * center, -1, keepdims=True) + norm_eps)


def rms_norm(values, norm_gain):
    return values * lax.rsqrt(jnp.mean(values * values, -1, keepdims=True) + norm_eps) * norm_gain


def body(inputs, modulation, w_qkv, w_attn_out, qk_gain, final_mod, w_final, w_embed, latent):
    head_dim = qk_gain.shape[2]
    x_rows = inputs[0]
    samples = x_rows.shape[0]
    mod_rows = modulation[0]
    x_float = x_rows.astype(jnp.float32)
    x_mod = (
        layer_norm(x_float) * (1.0 + mod_rows[:, 1, None, :]) + mod_rows[:, 0, None, :]
    ).astype(jnp.bfloat16)
    weights = w_qkv[0]
    local_width = weights.shape[2]
    heads_local = local_width // head_dim
    norm_gains = qk_gain[0]
    scaling = head_dim ** (-0.5)
    mixed_rows = jnp.einsum(
        "srd,dje->srje",
        lax.all_gather(x_mod, "tp", axis=1, tiled=True),
        weights,
        preferred_element_type=jnp.float32,
    )
    unpacked = mixed_rows.reshape(
        mixed_rows.shape[0], mixed_rows.shape[1], 3, heads_local, head_dim
    )
    project_queried = rms_norm(unpacked[:, :, 0], norm_gains[0])
    keyed_rows = rms_norm(unpacked[:, :, 1], norm_gains[1])
    projected = jnp.stack([project_queried, keyed_rows, unpacked[:, :, 2]], 2).astype(jnp.bfloat16)
    queried = projected[:, :, 0]
    query_count = queried.shape[1]
    pairs = projected[:, :, 1:]
    start_max = jnp.full((samples, query_count, heads_local), -1e30, jnp.float32)
    shard_piece = lax.all_gather(pairs, "seq", axis=1, tiled=True)
    run_max = start_max
    scores = (
        jnp.einsum(
            "sqhd,skhd->sqhk", queried, shard_piece[:, :, 0], preferred_element_type=jnp.float32
        )
        * scaling
    )
    new_max = jnp.maximum(run_max, jnp.max(scores, -1))
    weight = jnp.exp(scores - new_max[..., None])
    run_sum = jnp.sum(weight, -1)
    summed = jnp.einsum(
        "sqhk,skhd->sqhd",
        weight.astype(jnp.bfloat16),
        shard_piece[:, :, 1],
        preferred_element_type=jnp.float32,
    )
    run_acc = summed
    run_max, run_sum, run_acc = (new_max, run_sum, run_acc)
    attended = (
        (run_acc / run_sum[..., None])
        .astype(jnp.bfloat16)
        .reshape(samples, query_count, local_width)
    )
    partial_out = jnp.einsum(
        "sqe,ed->sqd", attended, w_attn_out[0], preferred_element_type=jnp.float32
    )
    branch = lax.psum_scatter(
        partial_out.astype(jnp.bfloat16), "tp", scatter_dimension=1, tiled=True
    ).astype(jnp.float32)
    output = (x_float + mod_rows[:, 2, None, :] * branch).astype(jnp.bfloat16)
    final_in = (
        layer_norm(output.astype(jnp.float32)) * (1.0 + final_mod[:, 1, None, :])
        + final_mod[:, 0, None, :]
    ).astype(jnp.bfloat16)
    velocity = jnp.einsum("srd,dc->scr", final_in, w_final, preferred_element_type=jnp.float32)
    advanced = latent + step_size * velocity
    last_comp = lax.axis_size("comp") - 1
    position = lax.axis_index("comp")
    shared = broadcast(
        jnp.stack([velocity, advanced]).astype(jnp.bfloat16), "comp", last_comp
    ).astype(jnp.float32)
    embedded = jnp.einsum(
        "scr,cd->srd", advanced.astype(jnp.bfloat16), w_embed, preferred_element_type=jnp.float32
    ).astype(jnp.bfloat16)
    sending = jnp.where(position == last_comp, embedded, output)
    handed = shifted(sending, "comp", 1)
    return (handed[None], shared[0], shared[1])


def by_clip(inputs, modulation, w_qkv, w_attn_out, qk_gain, final_mod, w_final, w_embed, latent):
    head_dim = qk_gain.shape[2]
    x_rows = inputs[0]
    samples, block, width = x_rows.shape
    clip = lax.axis_index("seq")
    comp = lax.axis_index("comp")
    comps = lax.axis_size("comp")
    tps = lax.axis_size("tp")
    sent = [
        lax.dynamic_index_in_dim(x_rows, lax.rem(clip + d, samples), 0, False)
        for d in range(samples)
    ]
    got = []
    for d in range(samples):
        route = [(i, (i + d) % samples) for i in range(samples)]
        got.append(lax.ppermute(sent[d], "seq", route) if d else sent[0])
    own_raw = jnp.concatenate(got, 0)
    mod = lax.dynamic_index_in_dim(modulation[0], clip, 0, False)
    own_float = own_raw.astype(jnp.float32)
    x_mod = (layer_norm(own_float) * (1.0 + mod[1]) + mod[0]).astype(jnp.bfloat16)
    x_full = lax.all_gather(x_mod, "tp", axis=0, tiled=True)
    rows = x_full.shape[0]
    weights = w_qkv[0]
    local_width = weights.shape[2]
    heads_local = local_width // head_dim
    mixed = jnp.einsum("rd,dje->jre", x_full, weights, preferred_element_type=jnp.float32)
    unpacked = mixed.reshape(3, rows, heads_local, head_dim)
    queried = rms_norm(unpacked[0], qk_gain[0, 0]).astype(jnp.bfloat16)
    keyed = rms_norm(unpacked[1], qk_gain[0, 1]).astype(jnp.bfloat16)
    valued = unpacked[2].astype(jnp.bfloat16)
    scores = jnp.einsum("qhd,khd->hqk", queried, keyed, preferred_element_type=jnp.float32) * (
        head_dim ** (-0.5)
    )
    weight = jnp.exp(scores - jnp.max(scores, -1, keepdims=True))
    total = jnp.sum(weight, -1)
    summed = jnp.einsum(
        "hqk,khd->qhd", weight.astype(jnp.bfloat16), valued, preferred_element_type=jnp.float32
    )
    attended = (summed / total.T[..., None]).astype(jnp.bfloat16).reshape(rows, local_width)
    partial_out = jnp.dot(attended, w_attn_out[0], preferred_element_type=jnp.float32)
    branch = lax.psum_scatter(
        partial_out.astype(jnp.bfloat16), "tp", scatter_dimension=0, tiled=True
    ).astype(jnp.float32)
    output = (own_float + mod[2] * branch).astype(jnp.bfloat16)
    return finish(output, samples, block, width, clip, comp, comps, final_mod, w_final, w_embed, latent)


def rolled(blocks, clip, samples):
    twice = jnp.concatenate([blocks, blocks], 0)
    return lax.dynamic_slice_in_dim(twice, lax.rem(samples - clip, samples), samples, 0)


def finish(output, samples, block, width, clip, comp, comps, final_mod, w_final, w_embed, latent):
    last = comps - 1
    fmod = lax.dynamic_index_in_dim(final_mod, clip, 0, False)
    final_in = (layer_norm(output.astype(jnp.float32)) * (1.0 + fmod[1]) + fmod[0]).astype(
        jnp.bfloat16
    )
    speed = jnp.dot(final_in, w_final, preferred_element_type=jnp.float32)
    channels = speed.shape[-1]
    slots = output.reshape(samples, block, width)
    speeds = speed.reshape(samples, block, channels)
    home, moved = [], []
    for d in range(samples):
        route = [
            (c * samples + i, (c + 1) * samples + (i - d) % samples)
            for c in range(comps - 1)
            for i in range(samples)
        ]
        home.append(lax.ppermute(slots[d], ("comp", "seq"), route))
        part = speeds[d]
        if d:
            part = lax.ppermute(part, "seq", [(i, (i - d) % samples) for i in range(samples)])
        moved.append(part)
    velocity = rolled(jnp.stack(moved), clip, samples)
    velocity = broadcast(velocity, "comp", last).transpose(0, 2, 1)
    advanced = latent + step_size * velocity
    embedded = jnp.einsum(
        "scr,cd->srd", advanced.astype(jnp.bfloat16), w_embed, preferred_element_type=jnp.float32
    ).astype(jnp.bfloat16)
    returned = rolled(jnp.stack(home), clip, samples)
    handed = jnp.where(comp == 0, embedded, returned)
    return (handed[None], velocity, advanced)


def plan(inputs, *rest):
    if inputs.shape[1] == lax.axis_size("seq"):
        return by_clip(inputs, *rest)
    return body(inputs, *rest)


def solution(mesh):
    in_specs = (
        P("comp", None, ("seq", "tp"), None),
        P("comp", None, None, None),
        P("comp", None, None, "tp"),
        P("comp", "tp", None),
        P("comp", None, None),
        P(),
        P(),
        P(),
        P(None, None, ("seq", "tp")),
    )
    out_specs = (
        P("comp", None, ("seq", "tp"), None),
        P(None, None, ("seq", "tp")),
        P(None, None, ("seq", "tp")),
    )
    return jax.shard_map(plan, mesh=mesh, in_specs=in_specs, out_specs=out_specs, check_vma=False)
```

```python
import jax
import jax.numpy as jnp
from jax import lax
from jax.experimental import pallas as pl
from jax.experimental.pallas import tpu as pltpu
from jax.sharding import PartitionSpec as P

MESH = pl.DeviceIdType.MESH

step_size = 0.02
norm_eps = 1e-06


def broadcast(block, axis, owner):
    block = jnp.where(lax.axis_index(axis) == owner, block, jnp.zeros_like(block))
    return lax.psum(block, axis)


def shifted(block, axis, distance):
    devices = range(lax.axis_size(axis))
    route = [((i - distance) % len(devices), i) for i in devices]
    return lax.ppermute(block, axis, route)


def layer_norm(values):
    center = values - jnp.mean(values, -1, keepdims=True)
    return center * lax.rsqrt(jnp.mean(center * center, -1, keepdims=True) + norm_eps)


def rms_norm(values, norm_gain):
    return values * lax.rsqrt(jnp.mean(values * values, -1, keepdims=True) + norm_eps) * norm_gain


def body(inputs, modulation, w_qkv, w_attn_out, qk_gain, final_mod, w_final, w_embed, latent):
    head_dim = qk_gain.shape[2]
    x_rows = inputs[0]
    samples = x_rows.shape[0]
    mod_rows = modulation[0]
    x_float = x_rows.astype(jnp.float32)
    x_mod = (
        layer_norm(x_float) * (1.0 + mod_rows[:, 1, None, :]) + mod_rows[:, 0, None, :]
    ).astype(jnp.bfloat16)
    weights = w_qkv[0]
    local_width = weights.shape[2]
    heads_local = local_width // head_dim
    norm_gains = qk_gain[0]
    scaling = head_dim ** (-0.5)
    mixed_rows = jnp.einsum(
        "srd,dje->srje",
        lax.all_gather(x_mod, "tp", axis=1, tiled=True),
        weights,
        preferred_element_type=jnp.float32,
    )
    unpacked = mixed_rows.reshape(
        mixed_rows.shape[0], mixed_rows.shape[1], 3, heads_local, head_dim
    )
    project_queried = rms_norm(unpacked[:, :, 0], norm_gains[0])
    keyed_rows = rms_norm(unpacked[:, :, 1], norm_gains[1])
    projected = jnp.stack([project_queried, keyed_rows, unpacked[:, :, 2]], 2).astype(jnp.bfloat16)
    queried = projected[:, :, 0]
    query_count = queried.shape[1]
    pairs = projected[:, :, 1:]
    start_max = jnp.full((samples, query_count, heads_local), -1e30, jnp.float32)
    shard_piece = lax.all_gather(pairs, "seq", axis=1, tiled=True)
    run_max = start_max
    scores = (
        jnp.einsum(
            "sqhd,skhd->sqhk", queried, shard_piece[:, :, 0], preferred_element_type=jnp.float32
        )
        * scaling
    )
    new_max = jnp.maximum(run_max, jnp.max(scores, -1))
    weight = jnp.exp(scores - new_max[..., None])
    run_sum = jnp.sum(weight, -1)
    summed = jnp.einsum(
        "sqhk,skhd->sqhd",
        weight.astype(jnp.bfloat16),
        shard_piece[:, :, 1],
        preferred_element_type=jnp.float32,
    )
    run_acc = summed
    run_max, run_sum, run_acc = (new_max, run_sum, run_acc)
    attended = (
        (run_acc / run_sum[..., None])
        .astype(jnp.bfloat16)
        .reshape(samples, query_count, local_width)
    )
    partial_out = jnp.einsum(
        "sqe,ed->sqd", attended, w_attn_out[0], preferred_element_type=jnp.float32
    )
    branch = lax.psum_scatter(
        partial_out.astype(jnp.bfloat16), "tp", scatter_dimension=1, tiled=True
    ).astype(jnp.float32)
    output = (x_float + mod_rows[:, 2, None, :] * branch).astype(jnp.bfloat16)
    final_in = (
        layer_norm(output.astype(jnp.float32)) * (1.0 + final_mod[:, 1, None, :])
        + final_mod[:, 0, None, :]
    ).astype(jnp.bfloat16)
    velocity = jnp.einsum("srd,dc->scr", final_in, w_final, preferred_element_type=jnp.float32)
    advanced = latent + step_size * velocity
    last_comp = lax.axis_size("comp") - 1
    position = lax.axis_index("comp")
    shared = broadcast(
        jnp.stack([velocity, advanced]).astype(jnp.bfloat16), "comp", last_comp
    ).astype(jnp.float32)
    embedded = jnp.einsum(
        "scr,cd->srd", advanced.astype(jnp.bfloat16), w_embed, preferred_element_type=jnp.float32
    ).astype(jnp.bfloat16)
    sending = jnp.where(position == last_comp, embedded, output)
    handed = shifted(sending, "comp", 1)
    return (handed[None], shared[0], shared[1])


def exchange_kernel(x_ref, own_ref, other_ref, send, recv, fsend, frecv, lsem):
    count = x_ref.shape[0]
    clip = lax.axis_index("seq")
    mate = 1 - lax.axis_index("tp")
    barrier = pltpu.get_barrier_semaphore()
    for d in range(1, count):
        pl.semaphore_signal(
            barrier, inc=1, device_id={"seq": lax.rem(clip + d, count)}, device_id_type=MESH
        )
    pl.semaphore_signal(barrier, inc=1, device_id={"tp": mate}, device_id_type=MESH)
    pl.semaphore_wait(barrier, count)
    copies = [None]
    for d in range(1, count):
        to = lax.rem(clip + d, count)
        copy = pltpu.make_async_remote_copy(
            src_ref=x_ref.at[to],
            dst_ref=own_ref.at[d],
            send_sem=send.at[d],
            recv_sem=recv.at[d],
            device_id={"seq": to},
            device_id_type=MESH,
        )
        copies.append(copy)

    def forward(d, source):
        copy = pltpu.make_async_remote_copy(
            src_ref=source,
            dst_ref=other_ref.at[d],
            send_sem=fsend.at[d],
            recv_sem=frecv.at[d],
            device_id={"tp": mate},
            device_id_type=MESH,
        )
        copy.start()
        return copy

    for d in range(1, count):
        copies[d].start()
    passed = [forward(0, x_ref.at[clip])]
    local = pltpu.make_async_copy(x_ref.at[clip], own_ref.at[0], lsem)
    local.start()
    order = []
    for d in range(1, count // 2 + 1):
        order += [d] if 2 * d == count else [d, count - d]
    for d in order:
        copies[d].wait_recv()
        passed.append(forward(d, own_ref.at[d]))
    local.wait()
    for copy in passed:
        copy.wait()
    for d in range(1, count):
        copies[d].wait_send()


def exchange(x_rows):
    count = x_rows.shape[0]
    return pl.pallas_call(
        exchange_kernel,
        out_shape=[jax.ShapeDtypeStruct(x_rows.shape, x_rows.dtype)] * 2,
        in_specs=[pl.BlockSpec(memory_space=pl.ANY)],
        out_specs=[pl.BlockSpec(memory_space=pl.ANY)] * 2,
        scratch_shapes=[pltpu.SemaphoreType.DMA((count,))] * 4 + [pltpu.SemaphoreType.DMA],
        compiler_params=pltpu.CompilerParams(collective_id=0, has_side_effects=True),
        name="exchange",
    )(x_rows)


def attention_kernel(mixed_ref, gain_ref, out_ref, q_ref, k_ref, v_ref):
    rows, head_dim = q_ref.shape
    scaling = head_dim ** (-0.5)
    q_ref[...] = rms_norm(mixed_ref[0], gain_ref[0:1, :]).astype(jnp.bfloat16)
    k_ref[...] = rms_norm(mixed_ref[1], gain_ref[1:2, :]).astype(jnp.bfloat16)
    v_ref[...] = mixed_ref[2].astype(jnp.bfloat16)
    step = min(256, rows)
    for at in range(0, rows, step):
        scores = lax.dot_general(
            q_ref[at : at + step, :],
            k_ref[...],
            (((1,), (1,)), ((), ())),
            preferred_element_type=jnp.float32,
        )
        scores = scores * scaling
        weight = jnp.exp(scores - jnp.max(scores, -1, keepdims=True))
        total = jnp.sum(weight, -1, keepdims=True)
        summed = jnp.dot(
            weight.astype(jnp.bfloat16), v_ref[...], preferred_element_type=jnp.float32
        )
        out_ref[at : at + step, :] = (summed / total).astype(jnp.bfloat16)


def attention(mixed, gains, head_dim):
    _, rows, width = mixed.shape
    return pl.pallas_call(
        attention_kernel,
        grid=(width // head_dim,),
        out_shape=jax.ShapeDtypeStruct((rows, width), jnp.bfloat16),
        in_specs=[
            pl.BlockSpec((3, rows, head_dim), lambda h: (0, 0, h)),
            pl.BlockSpec(gains.shape, lambda h: (0, 0)),
        ],
        out_specs=pl.BlockSpec((rows, head_dim), lambda h: (0, h)),
        scratch_shapes=[pltpu.VMEM((rows, head_dim), jnp.bfloat16)] * 3,
        compiler_params=pltpu.CompilerParams(vmem_limit_bytes=40 * 1024 * 1024),
        name="attention",
    )(mixed, gains)


def by_clip(inputs, modulation, w_qkv, w_attn_out, qk_gain, final_mod, w_final, w_embed, latent):
    head_dim = qk_gain.shape[2]
    x_rows = inputs[0]
    samples, block, width = x_rows.shape
    clip = lax.axis_index("seq")
    comp = lax.axis_index("comp")
    comps = lax.axis_size("comp")
    tps = lax.axis_size("tp")
    own_raw, other_raw = exchange(x_rows)
    own_raw = own_raw.reshape(samples * block, width)
    other_raw = other_raw.reshape(samples * block, width)
    mod = lax.dynamic_index_in_dim(modulation[0], clip, 0, False)
    own_float = own_raw.astype(jnp.float32)
    x_mod = (layer_norm(own_float) * (1.0 + mod[1]) + mod[0]).astype(jnp.bfloat16)
    other_mod = (layer_norm(other_raw.astype(jnp.float32)) * (1.0 + mod[1]) + mod[0]).astype(
        jnp.bfloat16
    )
    x_full = jnp.concatenate([x_mod, other_mod], 0)
    rows = x_full.shape[0]
    weights = w_qkv[0]
    local_width = weights.shape[2]
    mixed = jnp.einsum("rd,dje->jre", x_full, weights, preferred_element_type=jnp.float32)
    attended = attention(mixed, qk_gain[0], head_dim)
    half = rows // 2
    partner = jnp.dot(attended[half:], w_attn_out[0], preferred_element_type=jnp.float32)
    partner = lax.ppermute(partner.astype(jnp.bfloat16), "tp", [(0, 1), (1, 0)])
    mine = jnp.dot(attended[:half], w_attn_out[0], preferred_element_type=jnp.float32)
    branch = mine + partner.astype(jnp.float32)
    output = (own_float + mod[2] * branch).astype(jnp.bfloat16)
    return finish(output, samples, block, width, clip, comp, comps, final_mod, w_final, w_embed, latent)


def rolled(blocks, clip, samples):
    twice = jnp.concatenate([blocks, blocks], 0)
    return lax.dynamic_slice_in_dim(twice, lax.rem(samples - clip, samples), samples, 0)


def finish(output, samples, block, width, clip, comp, comps, final_mod, w_final, w_embed, latent):
    last = comps - 1
    fmod = lax.dynamic_index_in_dim(final_mod, clip, 0, False)
    final_in = (layer_norm(output.astype(jnp.float32)) * (1.0 + fmod[1]) + fmod[0]).astype(
        jnp.bfloat16
    )
    speed = jnp.dot(final_in, w_final, preferred_element_type=jnp.float32)
    channels = speed.shape[-1]
    slots = output.reshape(samples, block, width)
    speeds = speed.reshape(samples, block, channels)
    home, moved = [], []
    for d in range(samples):
        route = [
            (c * samples + i, (c + 1) * samples + (i - d) % samples)
            for c in range(comps - 1)
            for i in range(samples)
        ]
        home.append(lax.ppermute(slots[d], ("comp", "seq"), route))
        part = speeds[d]
        if d:
            part = lax.ppermute(part, "seq", [(i, (i - d) % samples) for i in range(samples)])
        moved.append(part)
    velocity = rolled(jnp.stack(moved), clip, samples)
    velocity = broadcast(velocity, "comp", last).transpose(0, 2, 1)
    advanced = latent + step_size * velocity
    embedded = jnp.einsum(
        "scr,cd->srd", advanced.astype(jnp.bfloat16), w_embed, preferred_element_type=jnp.float32
    ).astype(jnp.bfloat16)
    returned = rolled(jnp.stack(home), clip, samples)
    handed = jnp.where(comp == 0, embedded, returned)
    return (handed[None], velocity, advanced)


def plan(inputs, *rest):
    square = inputs.shape[1] == lax.axis_size("seq")
    if square and lax.axis_size("tp") == 2 and lax.axis_size("comp") == 2:
        return by_clip(inputs, *rest)
    return body(inputs, *rest)


def solution(mesh):
    in_specs = (
        P("comp", None, ("seq", "tp"), None),
        P("comp", None, None, None),
        P("comp", None, None, "tp"),
        P("comp", "tp", None),
        P("comp", None, None),
        P(),
        P(),
        P(),
        P(None, None, ("seq", "tp")),
    )
    out_specs = (
        P("comp", None, ("seq", "tp"), None),
        P(None, None, ("seq", "tp")),
        P(None, None, ("seq", "tp")),
    )
    return jax.shard_map(plan, mesh=mesh, in_specs=in_specs, out_specs=out_specs, check_vma=False)
```

```python
import functools

import jax
import jax.numpy as jnp
from jax import lax
from jax.experimental import pallas as pl
from jax.experimental.pallas import tpu as pltpu
from jax.sharding import PartitionSpec as P

MESH = pl.DeviceIdType.MESH

step_size = 0.02
norm_eps = 1e-06


def broadcast(block, axis, owner):
    block = jnp.where(lax.axis_index(axis) == owner, block, jnp.zeros_like(block))
    return lax.psum(block, axis)


def shifted(block, axis, distance):
    devices = range(lax.axis_size(axis))
    route = [((i - distance) % len(devices), i) for i in devices]
    return lax.ppermute(block, axis, route)


def layer_norm(values):
    center = values - jnp.mean(values, -1, keepdims=True)
    return center * lax.rsqrt(jnp.mean(center * center, -1, keepdims=True) + norm_eps)


def rms_norm(values, norm_gain):
    return values * lax.rsqrt(jnp.mean(values * values, -1, keepdims=True) + norm_eps) * norm_gain


def body(inputs, modulation, w_qkv, w_attn_out, qk_gain, final_mod, w_final, w_embed, latent):
    head_dim = qk_gain.shape[2]
    x_rows = inputs[0]
    samples = x_rows.shape[0]
    mod_rows = modulation[0]
    x_float = x_rows.astype(jnp.float32)
    x_mod = (
        layer_norm(x_float) * (1.0 + mod_rows[:, 1, None, :]) + mod_rows[:, 0, None, :]
    ).astype(jnp.bfloat16)
    weights = w_qkv[0]
    local_width = weights.shape[2]
    heads_local = local_width // head_dim
    norm_gains = qk_gain[0]
    scaling = head_dim ** (-0.5)
    mixed_rows = jnp.einsum(
        "srd,dje->srje",
        lax.all_gather(x_mod, "tp", axis=1, tiled=True),
        weights,
        preferred_element_type=jnp.float32,
    )
    unpacked = mixed_rows.reshape(
        mixed_rows.shape[0], mixed_rows.shape[1], 3, heads_local, head_dim
    )
    project_queried = rms_norm(unpacked[:, :, 0], norm_gains[0])
    keyed_rows = rms_norm(unpacked[:, :, 1], norm_gains[1])
    projected = jnp.stack([project_queried, keyed_rows, unpacked[:, :, 2]], 2).astype(jnp.bfloat16)
    queried = projected[:, :, 0]
    query_count = queried.shape[1]
    pairs = projected[:, :, 1:]
    start_max = jnp.full((samples, query_count, heads_local), -1e30, jnp.float32)
    shard_piece = lax.all_gather(pairs, "seq", axis=1, tiled=True)
    run_max = start_max
    scores = (
        jnp.einsum(
            "sqhd,skhd->sqhk", queried, shard_piece[:, :, 0], preferred_element_type=jnp.float32
        )
        * scaling
    )
    new_max = jnp.maximum(run_max, jnp.max(scores, -1))
    weight = jnp.exp(scores - new_max[..., None])
    run_sum = jnp.sum(weight, -1)
    summed = jnp.einsum(
        "sqhk,skhd->sqhd",
        weight.astype(jnp.bfloat16),
        shard_piece[:, :, 1],
        preferred_element_type=jnp.float32,
    )
    run_acc = summed
    run_max, run_sum, run_acc = (new_max, run_sum, run_acc)
    attended = (
        (run_acc / run_sum[..., None])
        .astype(jnp.bfloat16)
        .reshape(samples, query_count, local_width)
    )
    partial_out = jnp.einsum(
        "sqe,ed->sqd", attended, w_attn_out[0], preferred_element_type=jnp.float32
    )
    branch = lax.psum_scatter(
        partial_out.astype(jnp.bfloat16), "tp", scatter_dimension=1, tiled=True
    ).astype(jnp.float32)
    output = (x_float + mod_rows[:, 2, None, :] * branch).astype(jnp.bfloat16)
    final_in = (
        layer_norm(output.astype(jnp.float32)) * (1.0 + final_mod[:, 1, None, :])
        + final_mod[:, 0, None, :]
    ).astype(jnp.bfloat16)
    velocity = jnp.einsum("srd,dc->scr", final_in, w_final, preferred_element_type=jnp.float32)
    advanced = latent + step_size * velocity
    last_comp = lax.axis_size("comp") - 1
    position = lax.axis_index("comp")
    shared = broadcast(
        jnp.stack([velocity, advanced]).astype(jnp.bfloat16), "comp", last_comp
    ).astype(jnp.float32)
    embedded = jnp.einsum(
        "scr,cd->srd", advanced.astype(jnp.bfloat16), w_embed, preferred_element_type=jnp.float32
    ).astype(jnp.bfloat16)
    sending = jnp.where(position == last_comp, embedded, output)
    handed = shifted(sending, "comp", 1)
    return (handed[None], shared[0], shared[1])


def exchange_kernel(x_ref, own_ref, other_ref, send, recv, fsend, frecv, lsem):
    count = x_ref.shape[0]
    clip = lax.axis_index("seq")
    mate = 1 - lax.axis_index("tp")
    barrier = pltpu.get_barrier_semaphore()
    for d in range(1, count):
        pl.semaphore_signal(
            barrier, inc=1, device_id={"seq": lax.rem(clip + d, count)}, device_id_type=MESH
        )
    pl.semaphore_signal(barrier, inc=1, device_id={"tp": mate}, device_id_type=MESH)
    pl.semaphore_wait(barrier, count)
    copies = [None]
    for d in range(1, count):
        to = lax.rem(clip + d, count)
        copy = pltpu.make_async_remote_copy(
            src_ref=x_ref.at[to],
            dst_ref=own_ref.at[d],
            send_sem=send.at[d],
            recv_sem=recv.at[d],
            device_id={"seq": to},
            device_id_type=MESH,
        )
        copies.append(copy)

    def forward(d, source):
        copy = pltpu.make_async_remote_copy(
            src_ref=source,
            dst_ref=other_ref.at[d],
            send_sem=fsend.at[d],
            recv_sem=frecv.at[d],
            device_id={"tp": mate},
            device_id_type=MESH,
        )
        copy.start()
        return copy

    for d in range(1, count):
        copies[d].start()
    passed = [forward(0, x_ref.at[clip])]
    local = pltpu.make_async_copy(x_ref.at[clip], own_ref.at[0], lsem)
    local.start()
    order = []
    for d in range(1, count // 2 + 1):
        order += [d] if 2 * d == count else [d, count - d]
    for d in order:
        copies[d].wait_recv()
        passed.append(forward(d, own_ref.at[d]))
    local.wait()
    for copy in passed:
        copy.wait()
    for d in range(1, count):
        copies[d].wait_send()


def exchange(x_rows):
    count = x_rows.shape[0]
    return pl.pallas_call(
        exchange_kernel,
        out_shape=[jax.ShapeDtypeStruct(x_rows.shape, x_rows.dtype)] * 2,
        in_specs=[pl.BlockSpec(memory_space=pl.ANY)],
        out_specs=[pl.BlockSpec(memory_space=pl.ANY)] * 2,
        scratch_shapes=[pltpu.SemaphoreType.DMA((count,))] * 4 + [pltpu.SemaphoreType.DMA],
        compiler_params=pltpu.CompilerParams(collective_id=0, has_side_effects=True),
        name="exchange",
    )(x_rows)


def project_kernel(own_ref, other_ref, mod_ref, w_ref, gain_ref, out_ref, x_ref):
    half = own_ref.shape[0]
    head_dim = gain_ref.shape[1]
    step = min(64, half)

    @pl.when(pl.program_id(0) == 0)
    def _():
        for at, source in ((0, own_ref), (half, other_ref)):

            def modulate(i, carry):
                r = pl.multiple_of(i * step, step)
                rows = layer_norm(source[pl.ds(r, step), :].astype(jnp.float32))
                rows = rows * (1.0 + mod_ref[1:2, :]) + mod_ref[0:1, :]
                x_ref[pl.ds(at + r, step), :] = rows.astype(jnp.bfloat16)
                return carry

            lax.fori_loop(0, half // step, modulate, 0)

    for j in range(3):
        mixed = jnp.dot(x_ref[...], w_ref[j], preferred_element_type=jnp.float32)
        for h in range(mixed.shape[1] // head_dim):
            part = mixed[:, h * head_dim : (h + 1) * head_dim]
            if j < 2:
                part = rms_norm(part, gain_ref[j : j + 1, :])
            out_ref[j, :, h * head_dim : (h + 1) * head_dim] = part.astype(jnp.bfloat16)


def project(own_raw, other_raw, mod, weights, gains):
    half, width = own_raw.shape
    local = weights.shape[2]
    head_dim = gains.shape[1]
    tile = 2 * head_dim if local % (2 * head_dim) == 0 else head_dim
    once = pl.Buffered(1)
    return pl.pallas_call(
        project_kernel,
        grid=(local // tile,),
        out_shape=jax.ShapeDtypeStruct((3, 2 * half, local), jnp.bfloat16),
        in_specs=[
            pl.BlockSpec((half, width), lambda h: (0, 0), pipeline_mode=once),
            pl.BlockSpec((half, width), lambda h: (0, 0), pipeline_mode=once),
            pl.BlockSpec(mod.shape, lambda h: (0, 0)),
            pl.BlockSpec((3, width, tile), lambda h: (0, 0, h)),
            pl.BlockSpec(gains.shape, lambda h: (0, 0)),
        ],
        out_specs=pl.BlockSpec((3, 2 * half, tile), lambda h: (0, 0, h)),
        scratch_shapes=[pltpu.VMEM((2 * half, width), jnp.bfloat16)],
        compiler_params=pltpu.CompilerParams(vmem_limit_bytes=48 * 1024 * 1024),
        name="project",
    )(own_raw, other_raw, mod, weights, gains)


def attend_kernel(
    head_dim,
    qkv_ref,
    gate_ref,
    fmod_ref,
    w_final_ref,
    w_out_hbm,
    raw_hbm,
    home_ref,
    vel_ref,
    w_out_ref,
    raw_ref,
    att_ref,
    acc_ref,
    give_ref,
    take_ref,
    out_ref,
    speed_ref,
    lsem,
    x_send,
    x_recv,
    h_send,
    h_recv,
    v_send,
    v_recv,
):
    count, block, width = out_ref.shape
    chunks, step, _ = give_ref.shape
    per = step // block
    half = chunks * step
    heads = att_ref.shape[1] // head_dim
    scaling = head_dim ** (-0.5)
    comp = lax.axis_index("comp")
    clip = lax.axis_index("seq")
    mate = 1 - lax.axis_index("tp")
    load_w = pltpu.make_async_copy(w_out_hbm, w_out_ref, lsem.at[0])
    load_raw = pltpu.make_async_copy(raw_hbm, raw_ref, lsem.at[1])
    load_w.start()
    load_raw.start()
    barrier = pltpu.get_barrier_semaphore()
    for d in range(count):
        at = lax.rem(clip + d, count)
        pl.semaphore_signal(
            barrier, inc=1, device_id={"comp": 1 - comp, "seq": at}, device_id_type=MESH
        )
        if d:
            pl.semaphore_signal(barrier, inc=1, device_id={"seq": at}, device_id_type=MESH)
    pl.semaphore_signal(barrier, inc=1, device_id={"tp": mate}, device_id_type=MESH)
    pl.semaphore_wait(barrier, 2 * count)

    def owner(d):
        return lax.rem(clip - d + count, count)

    def sender(d):
        return lax.rem(clip + d, count)

    def x_copy(c):
        return pltpu.make_async_remote_copy(
            src_ref=give_ref.at[c],
            dst_ref=take_ref.at[c],
            send_sem=x_send.at[c],
            recv_sem=x_recv.at[c],
            device_id={"tp": mate},
            device_id_type=MESH,
        )

    def h_copy(d, slot):
        return pltpu.make_async_remote_copy(
            src_ref=out_ref.at[d],
            dst_ref=home_ref.at[slot],
            send_sem=h_send.at[d],
            recv_sem=h_recv.at[d],
            device_id={"comp": 1, "seq": owner(d)},
            device_id_type=MESH,
        )

    def v_copy(d, to, slot):
        return pltpu.make_async_remote_copy(
            src_ref=speed_ref.at[d],
            dst_ref=vel_ref.at[slot],
            send_sem=v_send.at[to, d],
            recv_sem=v_recv.at[d],
            device_id={"comp": to, "seq": owner(d)},
            device_id_type=MESH,
        )

    keep = pltpu.make_async_copy(speed_ref.at[0], vel_ref.at[clip], lsem.at[2])

    def attend(r):
        for h in range(heads):
            lanes = slice(h * head_dim, (h + 1) * head_dim)
            scores = lax.dot_general(
                qkv_ref[0, pl.ds(r, step), lanes],
                qkv_ref[1, :, lanes],
                (((1,), (1,)), ((), ())),
                preferred_element_type=jnp.float32,
            )
            scores = scores * scaling
            weight = jnp.exp(scores - jnp.max(scores, -1, keepdims=True))
            total = jnp.sum(weight, -1, keepdims=True)
            summed = jnp.dot(
                weight.astype(jnp.bfloat16),
                qkv_ref[2, :, lanes],
                preferred_element_type=jnp.float32,
            )
            att_ref[:, lanes] = (summed / total).astype(jnp.bfloat16)

    def for_mate(c, carry):
        attend(pl.multiple_of(half + c * step, step))

        @pl.when(c == 0)
        def _():
            load_w.wait()

        give_ref[c] = jnp.dot(
            att_ref[...], w_out_ref[...], preferred_element_type=jnp.float32
        ).astype(jnp.bfloat16)
        x_copy(c).start()
        return carry

    lax.fori_loop(0, chunks, for_mate, 0)
    load_raw.wait()

    def for_self(c, carry):
        r = pl.multiple_of(c * step, step)
        attend(r)
        acc_ref[...] = jnp.dot(att_ref[...], w_out_ref[...], preferred_element_type=jnp.float32)
        x_copy(c).wait_recv()
        for b in range(per):
            d = c * per + b
            rows = slice(b * block, (b + 1) * block)
            branch = acc_ref[rows, :] + take_ref[c, rows, :].astype(jnp.float32)
            raw = raw_ref[d].astype(jnp.float32)
            out_ref[d] = (raw + gate_ref[...] * branch).astype(jnp.bfloat16)

            @pl.when(comp == 0)
            def _():
                h_copy(d, clip).start()

            @pl.when(comp == 1)
            def _():
                final_in = layer_norm(out_ref[d].astype(jnp.float32))
                final_in = final_in * (1.0 + fmod_ref[1:2, :]) + fmod_ref[0:1, :]
                speed_ref[d] = jnp.dot(
                    final_in.astype(jnp.bfloat16),
                    w_final_ref[...],
                    preferred_element_type=jnp.float32,
                )
                v_copy(d, 0, clip).start()

                @pl.when(d > 0)
                def _():
                    v_copy(d, 1, clip).start()

                @pl.when(d == 0)
                def _():
                    keep.start()

        return carry

    lax.fori_loop(0, chunks, for_self, 0)
    for c in range(chunks):
        x_copy(c).wait_send()

    @pl.when(comp == 0)
    def _():
        for d in range(count):
            h_copy(d, clip).wait_send()
            v_copy(d, 0, sender(d)).wait_recv()

    @pl.when(comp == 1)
    def _():
        keep.wait()
        for d in range(count):
            v_copy(d, 0, clip).wait_send()
            if d:
                v_copy(d, 1, clip).wait_send()
                v_copy(d, 1, sender(d)).wait_recv()
            h_copy(d, sender(d)).wait_recv()


def attend_and_return(qkv, gate, fmod, w_final, w_out, raw, head_dim):
    count, block, width = raw.shape
    local = qkv.shape[2]
    lanes = w_final.shape[1]
    chunks = count // 2
    step = 2 * block
    vmem = pl.BlockSpec(memory_space=pltpu.VMEM)
    hbm = pl.BlockSpec(memory_space=pl.ANY)
    dma = pltpu.SemaphoreType.DMA
    return pl.pallas_call(
        functools.partial(attend_kernel, head_dim),
        out_shape=[
            jax.ShapeDtypeStruct((count, block, width), jnp.bfloat16),
            jax.ShapeDtypeStruct((count, block, lanes), jnp.float32),
        ],
        in_specs=[vmem, vmem, vmem, vmem, hbm, hbm],
        out_specs=[hbm, hbm],
        scratch_shapes=[
            pltpu.VMEM(w_out.shape, jnp.bfloat16),
            pltpu.VMEM(raw.shape, jnp.bfloat16),
            pltpu.VMEM((step, local), jnp.bfloat16),
            pltpu.VMEM((step, width), jnp.float32),
            pltpu.VMEM((chunks, step, width), jnp.bfloat16),
            pltpu.VMEM((chunks, step, width), jnp.bfloat16),
            pltpu.VMEM((count, block, width), jnp.bfloat16),
            pltpu.VMEM((count, block, lanes), jnp.float32),
            dma((3,)),
            dma((chunks,)),
            dma((chunks,)),
            dma((count,)),
            dma((count,)),
            dma((2, count)),
            dma((count,)),
        ],
        compiler_params=pltpu.CompilerParams(
            collective_id=1, has_side_effects=True, vmem_limit_bytes=56 * 1024 * 1024
        ),
        name="attend",
    )(qkv, gate, fmod, w_final, w_out, raw)


def by_clip(inputs, modulation, w_qkv, w_attn_out, qk_gain, final_mod, w_final, w_embed, latent):
    head_dim = qk_gain.shape[2]
    x_rows = inputs[0]
    samples, block, width = x_rows.shape
    channels = w_final.shape[1]
    clip = lax.axis_index("seq")
    own_raw, other_raw = exchange(x_rows)
    mod = lax.dynamic_index_in_dim(modulation[0], clip, 0, False)
    fmod = lax.dynamic_index_in_dim(final_mod, clip, 0, False)
    qkv = project(
        own_raw.reshape(samples * block, width),
        other_raw.reshape(samples * block, width),
        mod,
        w_qkv[0].transpose(1, 0, 2),
        qk_gain[0],
    )
    padded = jnp.pad(w_final, ((0, 0), (0, -channels % 128)))
    home, speeds = attend_and_return(
        qkv, mod[2:3], fmod, padded, w_attn_out[0], own_raw, head_dim
    )
    velocity = speeds[:, :, :channels].transpose(0, 2, 1)
    advanced = latent + step_size * velocity
    embedded = jnp.einsum(
        "scr,cd->srd", advanced.astype(jnp.bfloat16), w_embed, preferred_element_type=jnp.float32
    ).astype(jnp.bfloat16)
    handed = jnp.where(lax.axis_index("comp") == 0, embedded, home)
    return (handed[None], velocity, advanced)


def plan(inputs, *rest):
    square = inputs.shape[1] == lax.axis_size("seq")
    if square and lax.axis_size("tp") == 2 and lax.axis_size("comp") == 2:
        return by_clip(inputs, *rest)
    return body(inputs, *rest)


def solution(mesh):
    in_specs = (
        P("comp", None, ("seq", "tp"), None),
        P("comp", None, None, None),
        P("comp", None, None, "tp"),
        P("comp", "tp", None),
        P("comp", None, None),
        P(),
        P(),
        P(),
        P(None, None, ("seq", "tp")),
    )
    out_specs = (
        P("comp", None, ("seq", "tp"), None),
        P(None, None, ("seq", "tp")),
        P(None, None, ("seq", "tp")),
    )
    return jax.shard_map(plan, mesh=mesh, in_specs=in_specs, out_specs=out_specs, check_vma=False)
```

```python
import functools
import math

import jax
import jax.numpy as jnp
from jax import lax
from jax.experimental import pallas as pl
from jax.experimental.pallas import tpu as pltpu
from jax.sharding import PartitionSpec as P

MESH = pl.DeviceIdType.MESH

step_size = 0.02
norm_eps = 1e-06


def broadcast(block, axis, owner):
    block = jnp.where(lax.axis_index(axis) == owner, block, jnp.zeros_like(block))
    return lax.psum(block, axis)


def shifted(block, axis, distance):
    devices = range(lax.axis_size(axis))
    route = [((i - distance) % len(devices), i) for i in devices]
    return lax.ppermute(block, axis, route)


def layer_norm(values):
    center = values - jnp.mean(values, -1, keepdims=True)
    return center * lax.rsqrt(jnp.mean(center * center, -1, keepdims=True) + norm_eps)


def rms_norm(values, norm_gain):
    return values * lax.rsqrt(jnp.mean(values * values, -1, keepdims=True) + norm_eps) * norm_gain


def body(inputs, modulation, w_qkv, w_attn_out, qk_gain, final_mod, w_final, w_embed, latent):
    head_dim = qk_gain.shape[2]
    x_rows = inputs[0]
    samples = x_rows.shape[0]
    mod_rows = modulation[0]
    x_float = x_rows.astype(jnp.float32)
    x_mod = (
        layer_norm(x_float) * (1.0 + mod_rows[:, 1, None, :]) + mod_rows[:, 0, None, :]
    ).astype(jnp.bfloat16)
    weights = w_qkv[0]
    local_width = weights.shape[2]
    heads_local = local_width // head_dim
    norm_gains = qk_gain[0]
    scaling = head_dim ** (-0.5)
    mixed_rows = jnp.einsum(
        "srd,dje->srje",
        lax.all_gather(x_mod, "tp", axis=1, tiled=True),
        weights,
        preferred_element_type=jnp.float32,
    )
    unpacked = mixed_rows.reshape(
        mixed_rows.shape[0], mixed_rows.shape[1], 3, heads_local, head_dim
    )
    project_queried = rms_norm(unpacked[:, :, 0], norm_gains[0])
    keyed_rows = rms_norm(unpacked[:, :, 1], norm_gains[1])
    projected = jnp.stack([project_queried, keyed_rows, unpacked[:, :, 2]], 2).astype(jnp.bfloat16)
    queried = projected[:, :, 0]
    query_count = queried.shape[1]
    pairs = projected[:, :, 1:]
    start_max = jnp.full((samples, query_count, heads_local), -1e30, jnp.float32)
    shard_piece = lax.all_gather(pairs, "seq", axis=1, tiled=True)
    run_max = start_max
    scores = (
        jnp.einsum(
            "sqhd,skhd->sqhk", queried, shard_piece[:, :, 0], preferred_element_type=jnp.float32
        )
        * scaling
    )
    new_max = jnp.maximum(run_max, jnp.max(scores, -1))
    weight = jnp.exp(scores - new_max[..., None])
    run_sum = jnp.sum(weight, -1)
    summed = jnp.einsum(
        "sqhk,skhd->sqhd",
        weight.astype(jnp.bfloat16),
        shard_piece[:, :, 1],
        preferred_element_type=jnp.float32,
    )
    run_acc = summed
    run_max, run_sum, run_acc = (new_max, run_sum, run_acc)
    attended = (
        (run_acc / run_sum[..., None])
        .astype(jnp.bfloat16)
        .reshape(samples, query_count, local_width)
    )
    partial_out = jnp.einsum(
        "sqe,ed->sqd", attended, w_attn_out[0], preferred_element_type=jnp.float32
    )
    branch = lax.psum_scatter(
        partial_out.astype(jnp.bfloat16), "tp", scatter_dimension=1, tiled=True
    ).astype(jnp.float32)
    output = (x_float + mod_rows[:, 2, None, :] * branch).astype(jnp.bfloat16)
    final_in = (
        layer_norm(output.astype(jnp.float32)) * (1.0 + final_mod[:, 1, None, :])
        + final_mod[:, 0, None, :]
    ).astype(jnp.bfloat16)
    velocity = jnp.einsum("srd,dc->scr", final_in, w_final, preferred_element_type=jnp.float32)
    advanced = latent + step_size * velocity
    last_comp = lax.axis_size("comp") - 1
    position = lax.axis_index("comp")
    shared = broadcast(
        jnp.stack([velocity, advanced]).astype(jnp.bfloat16), "comp", last_comp
    ).astype(jnp.float32)
    embedded = jnp.einsum(
        "scr,cd->srd", advanced.astype(jnp.bfloat16), w_embed, preferred_element_type=jnp.float32
    ).astype(jnp.bfloat16)
    sending = jnp.where(position == last_comp, embedded, output)
    handed = shifted(sending, "comp", 1)
    return (handed[None], shared[0], shared[1])


def exchange_kernel(x_ref, own_ref, other_ref, send, recv, fsend, frecv, lsem):
    count = x_ref.shape[0]
    clip = lax.axis_index("seq")
    mate = 1 - lax.axis_index("tp")
    barrier = pltpu.get_barrier_semaphore()
    for d in range(1, count):
        pl.semaphore_signal(
            barrier, inc=1, device_id={"seq": lax.rem(clip + d, count)}, device_id_type=MESH
        )
    pl.semaphore_signal(barrier, inc=1, device_id={"tp": mate}, device_id_type=MESH)
    pl.semaphore_wait(barrier, count)
    copies = [None]
    for d in range(1, count):
        to = lax.rem(clip + d, count)
        copy = pltpu.make_async_remote_copy(
            src_ref=x_ref.at[to],
            dst_ref=own_ref.at[d],
            send_sem=send.at[d],
            recv_sem=recv.at[d],
            device_id={"seq": to},
            device_id_type=MESH,
        )
        copies.append(copy)

    def forward(d, source):
        copy = pltpu.make_async_remote_copy(
            src_ref=source,
            dst_ref=other_ref.at[d],
            send_sem=fsend.at[d],
            recv_sem=frecv.at[d],
            device_id={"tp": mate},
            device_id_type=MESH,
        )
        copy.start()
        return copy

    for d in range(1, count):
        copies[d].start()
    passed = [forward(0, x_ref.at[clip])]
    local = pltpu.make_async_copy(x_ref.at[clip], own_ref.at[0], lsem)
    local.start()
    order = []
    for d in range(1, count // 2 + 1):
        order += [d] if 2 * d == count else [d, count - d]
    for d in order:
        copies[d].wait_recv()
        passed.append(forward(d, own_ref.at[d]))
    local.wait()
    for copy in passed:
        copy.wait()
    for d in range(1, count):
        copies[d].wait_send()


def exchange(x_rows):
    count = x_rows.shape[0]
    return pl.pallas_call(
        exchange_kernel,
        out_shape=[jax.ShapeDtypeStruct(x_rows.shape, x_rows.dtype)] * 2,
        in_specs=[pl.BlockSpec(memory_space=pl.ANY)],
        out_specs=[pl.BlockSpec(memory_space=pl.ANY)] * 2,
        scratch_shapes=[pltpu.SemaphoreType.DMA((count,))] * 4 + [pltpu.SemaphoreType.DMA],
        compiler_params=pltpu.CompilerParams(collective_id=0, has_side_effects=True),
        name="exchange",
    )(x_rows)


def project_kernel(own_ref, other_ref, mod_ref, w_ref, gain_ref, out_ref, x_ref):
    half = own_ref.shape[0]
    head_dim = gain_ref.shape[1]
    step = min(64, half)

    @pl.when(pl.program_id(0) == 0)
    def _():
        for at, source in ((0, own_ref), (half, other_ref)):

            def modulate(i, carry):
                r = pl.multiple_of(i * step, step)
                rows = layer_norm(source[pl.ds(r, step), :].astype(jnp.float32))
                rows = rows * (1.0 + mod_ref[1:2, :]) + mod_ref[0:1, :]
                x_ref[pl.ds(at + r, step), :] = rows.astype(jnp.bfloat16)
                return carry

            lax.fori_loop(0, half // step, modulate, 0)

    for j in range(3):
        mixed = jnp.dot(x_ref[...], w_ref[j], preferred_element_type=jnp.float32)
        for h in range(mixed.shape[1] // head_dim):
            part = mixed[:, h * head_dim : (h + 1) * head_dim]
            if j < 2:
                part = rms_norm(part, gain_ref[j : j + 1, :])
            out_ref[j, :, h * head_dim : (h + 1) * head_dim] = part.astype(jnp.bfloat16)


def project(own_raw, other_raw, mod, weights, gains):
    half, width = own_raw.shape
    local = weights.shape[2]
    head_dim = gains.shape[1]
    tile = 2 * head_dim if local % (2 * head_dim) == 0 else head_dim
    once = pl.Buffered(1)
    return pl.pallas_call(
        project_kernel,
        grid=(local // tile,),
        out_shape=jax.ShapeDtypeStruct((3, 2 * half, local), jnp.bfloat16),
        in_specs=[
            pl.BlockSpec((half, width), lambda h: (0, 0), pipeline_mode=once),
            pl.BlockSpec((half, width), lambda h: (0, 0), pipeline_mode=once),
            pl.BlockSpec(mod.shape, lambda h: (0, 0)),
            pl.BlockSpec((3, width, tile), lambda h: (0, 0, h)),
            pl.BlockSpec(gains.shape, lambda h: (0, 0)),
        ],
        out_specs=pl.BlockSpec((3, 2 * half, tile), lambda h: (0, 0, h)),
        scratch_shapes=[pltpu.VMEM((2 * half, width), jnp.bfloat16)],
        compiler_params=pltpu.CompilerParams(vmem_limit_bytes=48 * 1024 * 1024),
        name="project",
    )(own_raw, other_raw, mod, weights, gains)


def attend_kernel(
    head_dim,
    qkv_ref,
    gate_ref,
    fmod_ref,
    w_final_ref,
    w_out_hbm,
    raw_hbm,
    home_ref,
    vel_ref,
    w_out_ref,
    raw_ref,
    att_ref,
    acc_ref,
    give_ref,
    take_ref,
    out_ref,
    speed_ref,
    lsem,
    x_send,
    x_recv,
    h_send,
    h_recv,
    v_send,
    v_recv,
):
    count, block, width = out_ref.shape
    step = att_ref.shape[0]
    per = step // block
    chunks = count // per
    half = count * block
    heads = att_ref.shape[1] // head_dim
    scaling = head_dim ** (-0.5)
    comp = lax.axis_index("comp")
    clip = lax.axis_index("seq")
    mate = 1 - lax.axis_index("tp")
    load_w = pltpu.make_async_copy(w_out_hbm, w_out_ref, lsem.at[0])
    load_raw = pltpu.make_async_copy(raw_hbm, raw_ref, lsem.at[1])
    load_w.start()
    load_raw.start()
    barrier = pltpu.get_barrier_semaphore()
    for d in range(count):
        at = lax.rem(clip + d, count)
        pl.semaphore_signal(
            barrier, inc=1, device_id={"comp": 1 - comp, "seq": at}, device_id_type=MESH
        )
        if d:
            pl.semaphore_signal(barrier, inc=1, device_id={"seq": at}, device_id_type=MESH)
    pl.semaphore_signal(barrier, inc=1, device_id={"tp": mate}, device_id_type=MESH)
    pl.semaphore_wait(barrier, 2 * count)

    def owner(d):
        return lax.rem(clip - d + count, count)

    def sender(d):
        return lax.rem(clip + d, count)

    def x_copy(d):
        return pltpu.make_async_remote_copy(
            src_ref=give_ref.at[d],
            dst_ref=take_ref.at[d],
            send_sem=x_send.at[d],
            recv_sem=x_recv.at[d],
            device_id={"tp": mate},
            device_id_type=MESH,
        )

    def h_copy(d, slot):
        return pltpu.make_async_remote_copy(
            src_ref=out_ref.at[d],
            dst_ref=home_ref.at[slot],
            send_sem=h_send.at[d],
            recv_sem=h_recv.at[d],
            device_id={"comp": 1, "seq": owner(d)},
            device_id_type=MESH,
        )

    def v_copy(d, to, slot):
        return pltpu.make_async_remote_copy(
            src_ref=speed_ref.at[d],
            dst_ref=vel_ref.at[slot],
            send_sem=v_send.at[to, d],
            recv_sem=v_recv.at[d],
            device_id={"comp": to, "seq": owner(d)},
            device_id_type=MESH,
        )

    keep = pltpu.make_async_copy(speed_ref.at[0], vel_ref.at[clip], lsem.at[2])

    def attend(r):
        for h in range(heads):
            lanes = slice(h * head_dim, (h + 1) * head_dim)
            scores = lax.dot_general(
                qkv_ref[0, pl.ds(r, step), lanes],
                qkv_ref[1, :, lanes],
                (((1,), (1,)), ((), ())),
                preferred_element_type=jnp.float32,
            )
            scores = scores * scaling
            weight = jnp.exp(scores - jnp.max(scores, -1, keepdims=True))
            total = jnp.sum(weight, -1, keepdims=True)
            summed = jnp.dot(
                weight.astype(jnp.bfloat16),
                qkv_ref[2, :, lanes],
                preferred_element_type=jnp.float32,
            )
            att_ref[:, lanes] = (summed / total).astype(jnp.bfloat16)

    def for_mate(c, carry):
        attend(pl.multiple_of(half + c * step, step))

        @pl.when(c == 0)
        def _():
            load_w.wait()

        part = jnp.dot(att_ref[...], w_out_ref[...], preferred_element_type=jnp.float32)
        for b in range(per):
            give_ref[c * per + b] = part[b * block : (b + 1) * block].astype(jnp.bfloat16)
            x_copy(c * per + b).start()
        return carry

    lax.fori_loop(0, chunks, for_mate, 0)
    load_raw.wait()

    def for_self(c, carry):
        r = pl.multiple_of(c * step, step)
        attend(r)
        acc_ref[...] = jnp.dot(att_ref[...], w_out_ref[...], preferred_element_type=jnp.float32)
        for b in range(per):
            d = c * per + b
            x_copy(d).wait_recv()
            rows = slice(b * block, (b + 1) * block)
            branch = acc_ref[rows, :] + take_ref[d].astype(jnp.float32)
            raw = raw_ref[d].astype(jnp.float32)
            out_ref[d] = (raw + gate_ref[...] * branch).astype(jnp.bfloat16)

            @pl.when(comp == 0)
            def _():
                h_copy(d, clip).start()

            @pl.when(comp == 1)
            def _():
                final_in = layer_norm(out_ref[d].astype(jnp.float32))
                final_in = final_in * (1.0 + fmod_ref[1:2, :]) + fmod_ref[0:1, :]
                speed_ref[d] = jnp.dot(
                    final_in.astype(jnp.bfloat16),
                    w_final_ref[...],
                    preferred_element_type=jnp.float32,
                )
                v_copy(d, 0, clip).start()

                @pl.when(d > 0)
                def _():
                    v_copy(d, 1, clip).start()

                @pl.when(d == 0)
                def _():
                    keep.start()

        return carry

    lax.fori_loop(0, chunks, for_self, 0)
    for d in range(count):
        x_copy(d).wait_send()

    @pl.when(comp == 0)
    def _():
        for d in range(count):
            h_copy(d, clip).wait_send()
            v_copy(d, 0, sender(d)).wait_recv()

    @pl.when(comp == 1)
    def _():
        keep.wait()
        for d in range(count):
            v_copy(d, 0, clip).wait_send()
            if d:
                v_copy(d, 1, clip).wait_send()
                v_copy(d, 1, sender(d)).wait_recv()
            h_copy(d, sender(d)).wait_recv()


def attend_and_return(qkv, gate, fmod, w_final, w_out, raw, head_dim):
    count, block, width = raw.shape
    local = qkv.shape[2]
    lanes = w_final.shape[1]
    step = block * math.gcd(count, max(1, 256 // block))
    vmem = pl.BlockSpec(memory_space=pltpu.VMEM)
    hbm = pl.BlockSpec(memory_space=pl.ANY)
    dma = pltpu.SemaphoreType.DMA
    return pl.pallas_call(
        functools.partial(attend_kernel, head_dim),
        out_shape=[
            jax.ShapeDtypeStruct((count, block, width), jnp.bfloat16),
            jax.ShapeDtypeStruct((count, block, lanes), jnp.float32),
        ],
        in_specs=[vmem, vmem, vmem, vmem, hbm, hbm],
        out_specs=[hbm, hbm],
        scratch_shapes=[
            pltpu.VMEM(w_out.shape, jnp.bfloat16),
            pltpu.VMEM(raw.shape, jnp.bfloat16),
            pltpu.VMEM((step, local), jnp.bfloat16),
            pltpu.VMEM((step, width), jnp.float32),
            pltpu.VMEM((count, block, width), jnp.bfloat16),
            pltpu.VMEM((count, block, width), jnp.bfloat16),
            pltpu.VMEM((count, block, width), jnp.bfloat16),
            pltpu.VMEM((count, block, lanes), jnp.float32),
            dma((3,)),
            dma((count,)),
            dma((count,)),
            dma((count,)),
            dma((count,)),
            dma((2, count)),
            dma((count,)),
        ],
        compiler_params=pltpu.CompilerParams(
            collective_id=1, has_side_effects=True, vmem_limit_bytes=56 * 1024 * 1024
        ),
        name="attend",
    )(qkv, gate, fmod, w_final, w_out, raw)


def by_clip(inputs, modulation, w_qkv, w_attn_out, qk_gain, final_mod, w_final, w_embed, latent):
    head_dim = qk_gain.shape[2]
    x_rows = inputs[0]
    samples, block, width = x_rows.shape
    channels = w_final.shape[1]
    clip = lax.axis_index("seq")
    own_raw, other_raw = exchange(x_rows)
    mod = lax.dynamic_index_in_dim(modulation[0], clip, 0, False)
    fmod = lax.dynamic_index_in_dim(final_mod, clip, 0, False)
    qkv = project(
        own_raw.reshape(samples * block, width),
        other_raw.reshape(samples * block, width),
        mod,
        w_qkv[0].transpose(1, 0, 2),
        qk_gain[0],
    )
    padded = jnp.pad(w_final, ((0, 0), (0, -channels % 128)))
    home, speeds = attend_and_return(
        qkv, mod[2:3], fmod, padded, w_attn_out[0], own_raw, head_dim
    )
    velocity = speeds[:, :, :channels].transpose(0, 2, 1)
    advanced = latent + step_size * velocity
    embedded = jnp.einsum(
        "scr,cd->srd", advanced.astype(jnp.bfloat16), w_embed, preferred_element_type=jnp.float32
    ).astype(jnp.bfloat16)
    handed = jnp.where(lax.axis_index("comp") == 0, embedded, home)
    return (handed[None], velocity, advanced)


def plan(inputs, *rest):
    square = inputs.shape[1] == lax.axis_size("seq")
    if square and lax.axis_size("tp") == 2 and lax.axis_size("comp") == 2:
        return by_clip(inputs, *rest)
    return body(inputs, *rest)


def solution(mesh):
    in_specs = (
        P("comp", None, ("seq", "tp"), None),
        P("comp", None, None, None),
        P("comp", None, None, "tp"),
        P("comp", "tp", None),
        P("comp", None, None),
        P(),
        P(),
        P(),
        P(None, None, ("seq", "tp")),
    )
    out_specs = (
        P("comp", None, ("seq", "tp"), None),
        P(None, None, ("seq", "tp")),
        P(None, None, ("seq", "tp")),
    )
    return jax.shard_map(plan, mesh=mesh, in_specs=in_specs, out_specs=out_specs, check_vma=False)
```
